256 devices in a mesh: row: 8 (over y, core), col: 32 (over x, z).
Axes of the slice: x: 4, y: 4, z: 8, core: 2. Of those that a mesh axis runs over, the one named last changes fastest.
Arguments:
- momentum: float32 [8192, 26624], P('row', 'col'), may hold values from -6 to 6
- gradient: bfloat16 [8192, 26624], P('row', 'col'), may hold values from -6 to 6
- right_factor: float32 [26624, 128], P('col'), may hold values from -0.0390625 to 0.0390625
Outputs:
- new_momentum: float32 [8192, 26624], P('row', 'col')
- update: bfloat16 [8192, 26624], P('row', 'col')
The draws below stay inside these ranges and needn't reach their ends.
All inputs are finite; a program needn't handle non-finite values.
Results may differ from the reference program's by a relative error of at most 0.001.
Values sent between devices are 32-bit elements; how exact they have to be, the bound alone decides.
No kernel may reach another device: no remote copies, remote signals or barrier semaphores. Data moves between devices by JAX's collectives and lax.ppermute only.
A program may use at most 64 MiB of HBM per device.

```python
import jax
import jax.numpy as jnp
from jax import lax

ROWS = 8192
COLS = 26624
RANK = 128


def level_of(rng, dims, cuts, low, high):
    def one(axis_at, parts):
        heights = jax.random.uniform(jax.random.fold_in(jax.random.fold_in(rng, 6), axis_at), (parts,), jnp.float32, low / len(cuts), high / len(cuts))
        return jnp.repeat(jnp.exp(heights), dims[axis_at] // parts).reshape((-1,) + (1,) * (len(dims) - axis_at - 1))

    factor_of = one(*cuts[0])
    for cut in cuts[1:]:
        factor_of = factor_of * one(*cut)
    return factor_of


def scatter_about(rng, extent, spread, limit, shards=(), dtype=jnp.bfloat16):
    entries = spread * jax.random.normal(rng, extent, jnp.float32)
    if shards:
        entries = entries * level_of(rng, extent, shards, -0.22, 0.18)
    return jnp.clip(entries, -limit, limit).astype(dtype)


def setup_inputs(seed: int = 0) -> dict:
    keys = jax.random.split(jax.random.key(seed), 4)
    return {
        "momentum": scatter_about(keys[0], (ROWS, COLS), 1.0, 6.0, ((0, 8), (1, 32)), jnp.float32),
        "gradient": scatter_about(keys[1], (ROWS, COLS), 1.0, 6.0, ((0, 8), (1, 32))),
        "right_factor": scatter_about(keys[2], (COLS, RANK), COLS ** -0.5, 0.0390625, ((0, 32),), jnp.float32),
    }


def reference(momentum, gradient, right_factor):
    high = lax.Precision.HIGHEST
    blend = momentum + gradient.astype(jnp.float32)
    left = jnp.dot(blend, right_factor, precision=high)
    gram = jnp.dot(left.T, left, precision=high)
    lower = jnp.linalg.cholesky(gram)
    basis = lax.linalg.triangular_solve(lower, left, left_side=False, lower=True, transpose_a=True)
    across = jnp.dot(blend.T, basis, precision=high)
    colsq = lax.optimization_barrier(jnp.sum(across * across, axis=0))
    fresh = across / jnp.sqrt(colsq + 1e-06)
    new_momentum = blend - 0.05 * jnp.dot(basis, across.T, precision=high)
    scale_factor = (ROWS * COLS / RANK) ** 0.5
    update = (scale_factor * jnp.dot(basis, fresh.T, precision=high)).astype(jnp.bfloat16)
    return (new_momentum, update)
```

```python
import jax
import jax.numpy as jnp
from jax import lax
from jax.sharding import PartitionSpec as P

ROWS = 8192
COLS = 26624
RANK = 128
HIGH = lax.Precision.HIGHEST

OTHER_CORE = [(i, i ^ 1) for i in range(8)]
SAME_CORE = [[0, 2, 4, 6], [1, 3, 5, 7]]


def contract_first(first, second):
    return lax.dot_general(first, second, (((0,), (0,)), ((), ())), precision=HIGH)


def exchange(blocks, axis, groups=None):
    return lax.all_to_all(blocks, axis, 0, 0, axis_index_groups=groups)


def spread(block, count, axis, groups=None):
    return exchange(jnp.broadcast_to(block[None], (count,) + block.shape), axis, groups)


def sum_over_col(partial):
    rows = partial.shape[0] // 32
    mine = jnp.sum(exchange(partial.reshape(32, rows, RANK), "col"), axis=0)
    return spread(mine, 32, "col").reshape(partial.shape)


def sum_over_row(partial):
    half = partial.shape[0] // 2
    core = lax.rem(lax.axis_index("row"), 2)
    halves = partial.reshape(2, half, RANK)
    keep = lax.dynamic_index_in_dim(halves, core, 0, keepdims=False)
    give = lax.dynamic_index_in_dim(halves, 1 - core, 0, keepdims=False)
    keep = keep + lax.ppermute(give, "row", OTHER_CORE)
    mine = jnp.sum(exchange(keep.reshape(4, half // 4, RANK), "row", SAME_CORE), axis=0)
    keep = spread(mine, 4, "row", SAME_CORE).reshape(half, RANK)
    theirs = lax.ppermute(keep, "row", OTHER_CORE)
    first = jnp.where(core == 0, keep, theirs)
    second = jnp.where(core == 0, theirs, keep)
    return jnp.concatenate([first, second], axis=0)


def body(momentum, gradient, right_factor):
    blend = momentum + gradient.astype(jnp.float32)
    left = sum_over_col(jnp.dot(blend, right_factor, precision=HIGH))
    both = sum_over_row(jnp.concatenate([contract_first(blend, left), contract_first(left, left)], axis=0))
    weighted, gram = both[:832], both[832:]
    lower = jnp.linalg.cholesky(gram)
    inverse = lax.linalg.triangular_solve(lower, jnp.eye(RANK, dtype=jnp.float32), left_side=True, lower=True)
    basis = jnp.dot(left, inverse.T, precision=HIGH)
    across = jnp.dot(weighted, inverse.T, precision=HIGH)
    colsq = jnp.sum(across * across, axis=0, keepdims=True)
    colsq = jnp.sum(spread(colsq, 32, "col"), axis=0)
    fresh = across / jnp.sqrt(colsq + 1e-06)
    new_momentum = blend - 0.05 * jnp.dot(basis, across.T, precision=HIGH)
    scale_factor = (ROWS * COLS / RANK) ** 0.5
    update = (scale_factor * jnp.dot(basis, fresh.T, precision=HIGH)).astype(jnp.bfloat16)
    return (new_momentum, update)


def solution(mesh):
    in_specs = (P("row", "col"), P("row", "col"), P("col", None))
    out_specs = (P("row", "col"), P("row", "col"))
    return jax.shard_map(body, mesh=mesh, in_specs=in_specs, out_specs=out_specs, check_vma=False)
```

```python
import jax
import jax.numpy as jnp
from jax import lax
from jax.experimental import pallas as pl
from jax.experimental.pallas import tpu as pltpu
from jax.sharding import PartitionSpec as P

ROWS = 8192
COLS = 26624
RANK = 128
HIGH = lax.Precision.HIGHEST
F32 = jnp.float32
BF16 = jnp.bfloat16

C = 832
R = 1024
STEPS = 4
BLOCK = 16

CORE, NEAR, FAR = 1, 2, 6


def dot(first, second, dims=((1,), (0,)), precision=None):
    return lax.dot_general(first, second, (dims, ((), ())), precision=precision, preferred_element_type=F32)


def split(x):
    high = x.astype(BF16)
    return high, (x - high.astype(F32)).astype(BF16)


def params(mib):
    return pltpu.CompilerParams(vmem_limit_bytes=mib << 20)


def left_kernel(m_ref, g_ref, r_ref, left_ref, blend_ref, both_ref):
    @pl.when(pl.program_id(0) == 0)
    def _():
        high, low = split(r_ref[...].T)
        both_ref[:RANK] = high
        both_ref[RANK:] = low

    blend = m_ref[...] + g_ref[...].astype(F32)
    blend_ref[...] = blend
    high, low = split(blend)
    wide = dot(both_ref[...], high)
    left_ref[...] = (wide[:RANK] + wide[RANK:] + dot(both_ref[:RANK], low)).T


def left_of(m, g, r):
    width = R // STEPS
    return pl.pallas_call(
        left_kernel,
        grid=(STEPS,),
        in_specs=[
            pl.BlockSpec((C, width), lambda i: (0, i)),
            pl.BlockSpec((C, width), lambda i: (0, i)),
            pl.BlockSpec((C, RANK), lambda i: (0, 0)),
        ],
        out_specs=[
            pl.BlockSpec((width, RANK), lambda i: (i, 0)),
            pl.BlockSpec((C, width), lambda i: (0, i)),
        ],
        out_shape=[jax.ShapeDtypeStruct((R, RANK), F32), jax.ShapeDtypeStruct((C, R), F32)],
        scratch_shapes=[pltpu.VMEM((2 * RANK, C), BF16)],
        compiler_params=params(24),
        cost_estimate=pl.CostEstimate(flops=6 * R * C * RANK, bytes_accessed=R * C * 10, transcendentals=0),
        name="left_part",
    )(m, g, r)


def gram_kernel(left_ref, out_ref):
    left = left_ref[...]
    out_ref[...] = dot(left, left, ((0,), (0,)), HIGH)


def gram_of(left):
    return pl.pallas_call(
        gram_kernel,
        out_shape=jax.ShapeDtypeStruct((RANK, RANK), F32),
        compiler_params=params(16),
        cost_estimate=pl.CostEstimate(flops=12 * R * RANK * RANK, bytes_accessed=R * RANK * 4, transcendentals=0),
        name="gram_part",
    )(left)


def weighted_kernel(blend_ref, left_ref, out_ref, both_ref):
    @pl.when(pl.program_id(0) == 0)
    def _():
        high, low = split(left_ref[...])
        both_ref[:, :RANK] = high
        both_ref[:, RANK:] = low

    high, low = split(blend_ref[...])
    wide = dot(high, both_ref[...])
    out_ref[...] = wide[:, :RANK] + wide[:, RANK:] + dot(low, both_ref[:, :RANK])


def weighted_of(blend, left):
    height = C // STEPS
    return pl.pallas_call(
        weighted_kernel,
        grid=(STEPS,),
        in_specs=[
            pl.BlockSpec((height, R), lambda i: (i, 0)),
            pl.BlockSpec((R, RANK), lambda i: (0, 0)),
        ],
        out_specs=pl.BlockSpec((height, RANK), lambda i: (i, 0)),
        out_shape=jax.ShapeDtypeStruct((C, RANK), F32),
        scratch_shapes=[pltpu.VMEM((R, 2 * RANK), BF16)],
        compiler_params=params(16),
        cost_estimate=pl.CostEstimate(flops=6 * R * C * RANK, bytes_accessed=R * C * 4, transcendentals=0),
        name="weighted_part",
    )(blend, left)


def inverse_kernel(gram_ref, out_ref, work_ref):
    n, b = RANK, BLOCK
    row = lax.broadcasted_iota(jnp.int32, (n, n), 0)
    column = lax.broadcasted_iota(jnp.int32, (n, n), 1)
    work_ref[:, :n] = gram_ref[...]
    work_ref[:, n:] = jnp.where(row == column, 1.0, 0.0)
    place = lax.broadcasted_iota(jnp.int32, (b, n), 0)
    for o in range(0, n, b):
        upper, inverse = work_ref[o : o + b, :n], work_ref[o : o + b, n:]
        columns = [jnp.broadcast_to(upper[:, o + j : o + j + 1], (b, n)) for j in range(b)]
        pivots = jnp.zeros((b, n), F32)
        for i in range(b):
            pivot = 1.0 / jnp.broadcast_to(columns[i][i : i + 1], (b, n))
            pivots = jnp.where(place == i, pivot, pivots)
            if i + 1 < b:
                factor = jnp.where(place > i, columns[i] * pivot, 0.0)
                for j in range(i + 1, b):
                    columns[j] = columns[j] - factor * columns[j][i : i + 1]
                upper = upper - factor * upper[i : i + 1]
                inverse = inverse - factor * inverse[i : i + 1]
        root = jnp.sqrt(pivots)
        upper, inverse = upper * root, inverse * root
        out_ref[o : o + b] = inverse
        if o + b < n:
            done = jnp.concatenate([upper, inverse], axis=1)
            work_ref[o + b :] -= dot(upper[:, o + b :], done, ((0,), (0,)), HIGH)


def inverse_of(gram):
    return pl.pallas_call(
        inverse_kernel,
        out_shape=jax.ShapeDtypeStruct((RANK, RANK), F32),
        scratch_shapes=[pltpu.VMEM((RANK, 2 * RANK), F32)],
        compiler_params=params(16),
        cost_estimate=pl.CostEstimate(flops=6 << 30, bytes_accessed=1 << 17, transcendentals=0),
        name="inverse_factor",
    )(gram)


def across_kernel(weighted_ref, inverse_ref, across_ref, colsq_ref):
    across = dot(weighted_ref[...], inverse_ref[...], ((1,), (1,)), HIGH)
    across_ref[...] = across
    colsq_ref[...] = jnp.broadcast_to(jnp.sum(across * across, axis=0, keepdims=True), colsq_ref.shape)


def across_of(weighted, inverse):
    return pl.pallas_call(
        across_kernel,
        out_shape=[jax.ShapeDtypeStruct((C, RANK), F32), jax.ShapeDtypeStruct((32, RANK), F32)],
        compiler_params=params(16),
        cost_estimate=pl.CostEstimate(flops=12 * C * RANK * RANK, bytes_accessed=C * RANK * 8, transcendentals=0),
        name="across_part",
    )(weighted, inverse)


def momentum_kernel(blend_ref, left_ref, inverse_ref, across_ref, new_ref, basis_ref):
    @pl.when(pl.program_id(0) == 0)
    def _():
        high, low = split(dot(inverse_ref[...], left_ref[...], ((1,), (1,)), HIGH))
        basis_ref[:RANK] = high
        basis_ref[RANK:] = low

    wide = jnp.concatenate(split(across_ref[...] * 0.05), axis=1)
    high = basis_ref[:RANK]
    new_ref[...] = blend_ref[...] - dot(wide, jnp.concatenate([high, high], axis=0))


def momentum_of(blend, left, inverse, across):
    height = C // STEPS
    return pl.pallas_call(
        momentum_kernel,
        grid=(STEPS,),
        in_specs=[
            pl.BlockSpec((height, R), lambda i: (i, 0)),
            pl.BlockSpec((R, RANK), lambda i: (0, 0)),
            pl.BlockSpec((RANK, RANK), lambda i: (0, 0)),
            pl.BlockSpec((height, RANK), lambda i: (i, 0)),
        ],
        out_specs=[
            pl.BlockSpec((height, R), lambda i: (i, 0)),
            pl.BlockSpec((2 * RANK, R), lambda i: (0, 0)),
        ],
        out_shape=[jax.ShapeDtypeStruct((C, R), F32), jax.ShapeDtypeStruct((2 * RANK, R), BF16)],
        compiler_params=params(24),
        cost_estimate=pl.CostEstimate(flops=4 * R * C * RANK, bytes_accessed=R * C * 8, transcendentals=0),
        name="new_momentum",
    )(blend, left, inverse, across)


def update_kernel(across_ref, colsq_ref, basis_ref, update_ref):
    colsq = jnp.sum(colsq_ref[...], axis=0, keepdims=True)
    scale_factor = (ROWS * COLS / RANK) ** 0.5
    high, low = split(across_ref[...] * (scale_factor / jnp.sqrt(colsq + 1e-06)))
    basis_high, basis_low = basis_ref[:RANK], basis_ref[RANK:]
    wide = jnp.concatenate([high, low], axis=1)
    product = dot(wide, jnp.concatenate([basis_high, basis_high], axis=0)) + dot(high, basis_low)
    update_ref[...] = product.astype(BF16)


def update_of(across, colsq, basis):
    height = C // STEPS
    return pl.pallas_call(
        update_kernel,
        grid=(STEPS,),
        in_specs=[
            pl.BlockSpec((height, RANK), lambda i: (i, 0)),
            pl.BlockSpec((32, RANK), lambda i: (0, 0)),
            pl.BlockSpec((2 * RANK, R), lambda i: (0, 0)),
        ],
        out_specs=pl.BlockSpec((height, R), lambda i: (i, 0)),
        out_shape=jax.ShapeDtypeStruct((C, R), BF16),
        compiler_params=params(16),
        cost_estimate=pl.CostEstimate(flops=6 * R * C * RANK, bytes_accessed=R * C * 2, transcendentals=0),
        name="update",
    )(across, colsq, basis)


def exchange(blocks, axis):
    return lax.all_to_all(blocks, axis, 0, 0)


def sum_over_col(partial):
    rows = partial.shape[0] // 32
    mine = jnp.sum(exchange(partial.reshape(32, rows, RANK), "col"), axis=0)
    return exchange(jnp.broadcast_to(mine[None], (32, rows, RANK)), "col").reshape(partial.shape)


def swap(x, flip):
    return lax.ppermute(x, "row", [(i, i ^ flip) for i in range(8)])


def sum_over_row(weighted, gram):
    core = lax.rem(lax.axis_index("row"), 2)
    gram = gram + swap(gram, CORE)
    halves = weighted.reshape(2, C // 2, RANK)
    keep = lax.dynamic_index_in_dim(halves, core, 0, keepdims=False)
    give = lax.dynamic_index_in_dim(halves, 1 - core, 0, keepdims=False)
    keep = keep + swap(give, CORE)
    gram = gram + swap(gram, NEAR)
    gram = gram + swap(gram, FAR)
    first, second = keep[: C // 4], keep[C // 4 :]
    first = first + swap(first, NEAR)
    second = second + swap(second, FAR)
    first = first + swap(first, FAR)
    second = second + swap(second, NEAR)
    keep = jnp.concatenate([first, second], axis=0)
    theirs = swap(keep, CORE)
    upper = jnp.where(core == 0, keep, theirs)
    lower = jnp.where(core == 0, theirs, keep)
    return jnp.concatenate([upper, lower], axis=0), gram


def body(momentum, gradient, right_factor):
    partial, blend = left_of(momentum.T, gradient.T, right_factor)
    left = sum_over_col(partial)
    weighted, gram = sum_over_row(weighted_of(blend, left), gram_of(left))
    inverse = inverse_of(gram)
    across, colsq = across_of(weighted, inverse)
    colsq = exchange(colsq.reshape(32, 1, RANK), "col").reshape(32, RANK)
    new_momentum, basis = momentum_of(blend, left, inverse, across)
    update = update_of(across, colsq, basis)
    return (new_momentum.T, update.T)


def solution(mesh):
    in_specs = (P("row", "col"), P("row", "col"), P("col", None))
    out_specs = (P("row", "col"), P("row", "col"))
    return jax.shard_map(body, mesh=mesh, in_specs=in_specs, out_specs=out_specs, check_vma=False)
```

```python
import jax
import jax.numpy as jnp
from jax import lax
from jax.experimental import pallas as pl
from jax.experimental.pallas import tpu as pltpu
from jax.sharding import PartitionSpec as P

ROWS = 8192
COLS = 26624
RANK = 128
HIGH = lax.Precision.HIGHEST
F32 = jnp.float32
BF16 = jnp.bfloat16

C = 832
R = 1024
DEEP = ((0, 64), (64, 320), (320, 576), (576, 832))
EVEN = tuple((n, n + 208) for n in range(0, C, 208))
BLOCK = 64

QUARTER = C // 4
PART = QUARTER + RANK // 2

CORE, NEAR, FAR = 1, 2, 6


def dot(first, second, dims=((1,), (0,)), precision=None):
    return lax.dot_general(first, second, (dims, ((), ())), precision=precision, preferred_element_type=F32)


def split(x):
    high = x.astype(BF16)
    return high, (x - high.astype(F32)).astype(BF16)


WHOLE = pl.BlockSpec(memory_space=pltpu.VMEM)
ANY = pl.BlockSpec(memory_space=pl.ANY)


def near(*arrays):
    return [pltpu.with_memory_space_constraint(x, pltpu.VMEM) for x in arrays]


def far(*arrays):
    return [pltpu.with_memory_space_constraint(x, pltpu.HBM) for x in arrays]


def params(mib):
    return pltpu.CompilerParams(vmem_limit_bytes=mib << 20)


def start_loads(sources, targets, groups, sems):
    copies = []
    for n, (start, stop) in enumerate(groups):
        rows = pl.ds(start, stop - start)
        pair = [
            pltpu.make_async_copy(source.at[rows], target.at[rows], sems.at[n, k])
            for k, (source, target) in enumerate(zip(sources, targets))
        ]
        for copy in pair:
            copy.start()
        copies.append(pair)
    return copies


def left_kernel(m_hbm, g_hbm, r_hbm, left_ref, m_ref, g_ref, r_ref, both_ref, sum_ref, sems, r_sem):
    first = pltpu.make_async_copy(r_hbm, r_ref, r_sem)
    first.start()
    loads = start_loads((m_hbm, g_hbm), (m_ref, g_ref), DEEP, sems)
    first.wait()
    high, low = split(r_ref[...].T)
    both_ref[:RANK] = high
    both_ref[RANK:] = low
    for n, (start, stop) in enumerate(DEEP):
        for copy in loads[n]:
            copy.wait()
        high, low = split(m_ref[start:stop] + g_ref[start:stop].astype(F32))
        wide = dot(both_ref[:, start:stop], high)
        part = wide[:RANK] + wide[RANK:] + dot(both_ref[:RANK, start:stop], low)
        sum_ref[...] = part if n == 0 else sum_ref[...] + part
    left_ref[...] = sum_ref[...].T


def left_of(m, g, r):
    return pl.pallas_call(
        left_kernel,
        in_specs=[ANY, ANY, ANY],
        out_specs=WHOLE,
        out_shape=pltpu.VMEM((R, RANK), F32),
        scratch_shapes=[
            pltpu.VMEM((C, R), F32),
            pltpu.VMEM((C, R), BF16),
            pltpu.VMEM((C, RANK), F32),
            pltpu.VMEM((2 * RANK, C), BF16),
            pltpu.VMEM((RANK, R), F32),
            pltpu.SemaphoreType.DMA((len(DEEP), 2)),
            pltpu.SemaphoreType.DMA,
        ],
        compiler_params=params(14),
        cost_estimate=pl.CostEstimate(flops=6 * R * C * RANK, bytes_accessed=R * C * 6, transcendentals=0),
        name="left_part",
    )(*far(m, g, r))


def spread_kernel(parts_ref, out_ref, token_ref):
    total = jnp.sum(parts_ref[...], axis=0, keepdims=True)
    out_ref[...] = jnp.broadcast_to(total, out_ref.shape)
    token_ref[...] = total[0, :8]


def sum_and_spread(parts):
    return pl.pallas_call(
        spread_kernel,
        out_shape=[pltpu.VMEM(parts.shape, F32), pltpu.VMEM((8, RANK), F32)],
        in_specs=[WHOLE],
        out_specs=[WHOLE, WHOLE],
        compiler_params=params(4),
        cost_estimate=pl.CostEstimate(flops=parts.size, bytes_accessed=8 * parts.size, transcendentals=0),
        name="sum_and_spread",
    )(*near(parts))


def split_kernel(m_hbm, g_hbm, token_ref, out_ref, m_ref, g_ref, sems):
    loads = start_loads((m_hbm, g_hbm), (m_ref, g_ref), EVEN, sems)
    for n, (start, stop) in enumerate(EVEN):
        for copy in loads[n]:
            copy.wait()
        high, low = split(m_ref[start:stop] + g_ref[start:stop].astype(F32))
        out_ref[start:stop] = high
        out_ref[C + start : C + stop] = low


def split_of(m, g, token):
    return pl.pallas_call(
        split_kernel,
        in_specs=[ANY, ANY, WHOLE],
        out_specs=WHOLE,
        out_shape=pltpu.VMEM((2 * C, R), BF16),
        scratch_shapes=[
            pltpu.VMEM((C, R), F32),
            pltpu.VMEM((C, R), BF16),
            pltpu.SemaphoreType.DMA((len(EVEN), 2)),
        ],
        compiler_params=params(8),
        cost_estimate=pl.CostEstimate(flops=4 * R * C, bytes_accessed=R * C * 10, transcendentals=0),
        name="split_blend",
    )(*far(m, g), *near(token))


def weighted_kernel(core_ref, left_ref, blend_ref, give_ref, first_ref, second_ref, both_ref):
    left = left_ref[...]
    high, low = split(left)
    both_ref[:, :RANK] = high
    both_ref[:, RANK:] = low
    rest = (left - high.astype(F32) - low.astype(F32)).astype(BF16)
    wide = dot(high, both_ref[...], ((0,), (0,)))
    mixed = wide[:, RANK:] + dot(high, rest, ((0,), (0,)))
    gram = wide[:, :RANK] + (mixed + mixed.T + dot(low, low, ((0,), (0,))))
    half = RANK // 2
    give_ref[QUARTER:PART] = gram[:half]
    give_ref[PART + QUARTER :] = gram[half:]
    first_ref[QUARTER:] = gram[:half]
    second_ref[QUARTER:] = gram[half:]
    mine, theirs = core_ref[0] * (C // 2), (1 - core_ref[0]) * (C // 2)

    def product(start):
        wide = dot(blend_ref[pl.ds(pl.multiple_of(start, 16), QUARTER)], both_ref[...])
        rest = dot(blend_ref[pl.ds(pl.multiple_of(C + start, 16), QUARTER)], both_ref[:, :RANK])
        return wide[:, :RANK] + wide[:, RANK:] + rest

    give_ref[:QUARTER] = product(theirs)
    give_ref[PART : PART + QUARTER] = product(theirs + QUARTER)
    first_ref[:QUARTER] = product(mine)
    second_ref[:QUARTER] = product(mine + QUARTER)


def weighted_of(core, left, blend):
    return pl.pallas_call(
        weighted_kernel,
        in_specs=[pl.BlockSpec(memory_space=pltpu.SMEM), WHOLE, WHOLE],
        out_specs=[WHOLE, WHOLE, WHOLE],
        out_shape=[pltpu.VMEM((2 * PART, RANK), F32)] + [pltpu.VMEM((PART, RANK), F32)] * 2,
        scratch_shapes=[pltpu.VMEM((R, 2 * RANK), BF16)],
        compiler_params=params(6),
        cost_estimate=pl.CostEstimate(flops=6 * R * C * RANK, bytes_accessed=R * C * 4, transcendentals=0),
        name="weighted_part",
    )(core, *near(left, blend))


def inverse_kernel(first_ref, second_ref, out_ref, work_ref):
    n, b, t = RANK, BLOCK, 8
    row = lax.broadcasted_iota(jnp.int32, (n, n), 0)
    column = lax.broadcasted_iota(jnp.int32, (n, n), 1)
    work_ref[: n // 2, :n] = first_ref[QUARTER:]
    work_ref[n // 2 :, :n] = second_ref[QUARTER:]
    work_ref[:, n:] = jnp.where(row == column, 1.0, 0.0)
    place = lax.broadcasted_iota(jnp.int32, (t, n), 0)
    for o in range(0, n, b):
        upper = [work_ref[o + k : o + k + t, :n] for k in range(0, b, t)]
        inverse = [work_ref[o + k : o + k + t, n:] for k in range(0, b, t)]
        pivots = []
        for k in range(b // t):
            below = range(k, b // t)
            at = o + k * t
            columns = {q: [jnp.broadcast_to(upper[q][:, at + j : at + j + 1], (t, n)) for j in range(t)] for q in below}
            held = jnp.zeros((t, n), F32)
            for i in range(t):
                pivot = 1.0 / jnp.broadcast_to(columns[k][i][i : i + 1], (t, n))
                held = jnp.where(place == i, pivot, held)
                line = [columns[k][j][i : i + 1] for j in range(t)]
                upper_line, inverse_line = upper[k][i : i + 1], inverse[k][i : i + 1]
                for q in below:
                    factor = columns[q][i] * pivot
                    if q == k:
                        factor = jnp.where(place > i, factor, 0.0)
                    for j in range(i + 1, t):
                        columns[q][j] = columns[q][j] - factor * line[j]
                    upper[q] = upper[q] - factor * upper_line
                    inverse[q] = inverse[q] - factor * inverse_line
            pivots.append(held)
        root = jnp.sqrt(jnp.concatenate(pivots, axis=0))
        upper_block = jnp.concatenate(upper, axis=0) * root
        inverse_block = jnp.concatenate(inverse, axis=0) * root
        out_ref[o : o + b] = inverse_block
        if o + b < n:
            done = jnp.concatenate([upper_block, inverse_block], axis=1)
            work_ref[o + b :] -= dot(upper_block[:, o + b :], done, ((0,), (0,)), HIGH)


def inverse_of(first, second):
    return pl.pallas_call(
        inverse_kernel,
        out_shape=pltpu.VMEM((RANK, RANK), F32),
        in_specs=[WHOLE, WHOLE],
        out_specs=WHOLE,
        scratch_shapes=[pltpu.VMEM((RANK, 2 * RANK), F32)],
        compiler_params=params(2),
        cost_estimate=pl.CostEstimate(flops=60 << 30, bytes_accessed=1 << 17, transcendentals=0),
        name="inverse_factor",
    )(*near(first, second))


def across_kernel(core_ref, first_ref, second_ref, other_ref, inverse_ref, across_ref, colsq_ref):
    high, low = split(inverse_ref[...].T)
    three = jnp.concatenate([high, high, low], axis=0)
    mine, theirs = core_ref[0] * (C // 2), (1 - core_ref[0]) * (C // 2)
    total = jnp.zeros((1, RANK), F32)
    for part, start in (
        (first_ref[:QUARTER], mine),
        (second_ref[:QUARTER], mine + QUARTER),
        (other_ref[...], theirs),
    ):
        high, low = split(part)
        part = dot(jnp.concatenate([high, low, high], axis=1), three)
        across_ref[pl.ds(pl.multiple_of(start, 8), part.shape[0])] = part
        total = total + jnp.sum(part * part, axis=0, keepdims=True)
    colsq_ref[...] = jnp.broadcast_to(total, colsq_ref.shape)


def across_of(core, first, second, other, inverse):
    return pl.pallas_call(
        across_kernel,
        in_specs=[pl.BlockSpec(memory_space=pltpu.SMEM), WHOLE, WHOLE, WHOLE, WHOLE],
        out_specs=[WHOLE, WHOLE],
        out_shape=[pltpu.VMEM((C, RANK), F32), pltpu.VMEM((32, RANK), F32)],
        compiler_params=params(4),
        cost_estimate=pl.CostEstimate(flops=12 * C * RANK * RANK, bytes_accessed=C * RANK * 8, transcendentals=0),
        name="across_part",
    )(core, *near(first, second, other, inverse))


def store(source, target, groups, sems, n):
    rows = pl.ds(groups[n][0], groups[n][1] - groups[n][0])
    copy = pltpu.make_async_copy(source.at[rows], target.at[rows], sems.at[n])
    copy.start()
    return copy


def momentum_kernel(m_hbm, g_hbm, left_ref, inverse_ref, across_ref, new_hbm, basis_ref, m_ref, g_ref, new_ref, sems, out_sems):
    loads = start_loads((m_hbm, g_hbm), (m_ref, g_ref), EVEN, sems)
    high, low = split(dot(inverse_ref[...], left_ref[...], ((1,), (1,)), HIGH))
    basis_ref[:RANK] = high
    basis_ref[RANK : 2 * RANK] = high
    basis_ref[2 * RANK :] = low
    stores = []
    for n, (start, stop) in enumerate(EVEN):
        for copy in loads[n]:
            copy.wait()
        wide = jnp.concatenate(split(across_ref[start:stop] * 0.05), axis=1)
        blend = m_ref[start:stop] + g_ref[start:stop].astype(F32)
        new_ref[start:stop] = blend - dot(wide, basis_ref[: 2 * RANK])
        stores.append(store(new_ref, new_hbm, EVEN, out_sems, n))
    for copy in stores:
        copy.wait()


def momentum_of(m, g, left, inverse, across):
    return pl.pallas_call(
        momentum_kernel,
        in_specs=[ANY, ANY, WHOLE, WHOLE, WHOLE],
        out_specs=[ANY, WHOLE],
        out_shape=[pltpu.HBM((C, R), F32), pltpu.VMEM((3 * RANK, R), BF16)],
        scratch_shapes=[
            pltpu.VMEM((C, R), F32),
            pltpu.VMEM((C, R), BF16),
            pltpu.VMEM((C, R), F32),
            pltpu.SemaphoreType.DMA((len(EVEN), 2)),
            pltpu.SemaphoreType.DMA((len(EVEN),)),
        ],
        compiler_params=params(14),
        cost_estimate=pl.CostEstimate(flops=4 * R * C * RANK, bytes_accessed=R * C * 10, transcendentals=0),
        name="new_momentum",
    )(*far(m, g), *near(left, inverse, across))


def update_kernel(across_ref, colsq_ref, basis_ref, update_hbm, update_ref, sems):
    colsq = jnp.sum(colsq_ref[...], axis=0, keepdims=True)
    scale = (ROWS * COLS / RANK) ** 0.5 / jnp.sqrt(colsq + 1e-06)
    stores = []
    for n, (start, stop) in enumerate(EVEN):
        high, low = split(across_ref[start:stop] * scale)
        product = dot(jnp.concatenate([high, low, high], axis=1), basis_ref[...])
        update_ref[start:stop] = product.astype(BF16)
        stores.append(store(update_ref, update_hbm, EVEN, sems, n))
    for copy in stores:
        copy.wait()


def update_of(across, colsq, basis):
    return pl.pallas_call(
        update_kernel,
        in_specs=[WHOLE, WHOLE, WHOLE],
        out_specs=ANY,
        out_shape=pltpu.HBM((C, R), BF16),
        scratch_shapes=[pltpu.VMEM((C, R), BF16), pltpu.SemaphoreType.DMA((len(EVEN),))],
        compiler_params=params(6),
        cost_estimate=pl.CostEstimate(flops=6 * R * C * RANK, bytes_accessed=R * C * 2, transcendentals=0),
        name="update",
    )(*near(across, colsq, basis))


def exchange(blocks, axis):
    return lax.all_to_all(blocks, axis, 0, 0)


def swap(x, flip):
    return lax.ppermute(x, "row", [(i, i ^ flip) for i in range(8)])


def body(momentum, gradient, right_factor):
    m, g = momentum.T, gradient.T
    core = lax.rem(lax.axis_index("row"), 2).astype(jnp.int32).reshape(1)
    partial = left_of(m, g, right_factor)
    parts = exchange(partial.reshape(32, R // 32, RANK), "col")
    spread, token = sum_and_spread(parts)
    left = exchange(spread, "col").reshape(R, RANK)
    blend = split_of(m, g, token)

    give, first, second = weighted_of(core, left, blend)
    given = swap(give, CORE)
    first, second = first + given[:PART], second + given[PART:]
    first, second = first + swap(first, NEAR), second + swap(second, FAR)
    first, second = first + swap(first, FAR), second + swap(second, NEAR)
    other = swap(jnp.concatenate([first[:QUARTER], second[:QUARTER]], axis=0), CORE)
    inverse = inverse_of(first, second)

    across, colsq = across_of(core, first, second, other, inverse)
    colsq = exchange(colsq.reshape(32, 1, RANK), "col").reshape(32, RANK)
    new_momentum, basis = momentum_of(m, g, left, inverse, across)
    update = update_of(across, colsq, basis)
    return (new_momentum.T, update.T)


def solution(mesh):
    in_specs = (P("row", "col"), P("row", "col"), P("col", None))
    out_specs = (P("row", "col"), P("row", "col"))
    return jax.shard_map(body, mesh=mesh, in_specs=in_specs, out_specs=out_specs, check_vma=False)
```

```python
import jax
import jax.numpy as jnp
from jax import lax
from jax.experimental import pallas as pl
from jax.experimental.pallas import tpu as pltpu
from jax.sharding import PartitionSpec as P

ROWS = 8192
COLS = 26624
RANK = 128
HIGH = lax.Precision.HIGHEST
F32 = jnp.float32
BF16 = jnp.bfloat16

C = 832
R = 1024
DEEP = ((0, 64), (64, 320), (320, 576), (576, 832))
EVEN = tuple((n, n + 208) for n in range(0, C, 208))
BLOCK = 64

HALF = C // 2
SMEM = pl.BlockSpec(memory_space=pltpu.SMEM)


def dot(first, second, dims=((1,), (0,)), precision=None):
    return lax.dot_general(first, second, (dims, ((), ())), precision=precision, preferred_element_type=F32)


def split(x):
    high = x.astype(BF16)
    return high, (x - high.astype(F32)).astype(BF16)


WHOLE = pl.BlockSpec(memory_space=pltpu.VMEM)
ANY = pl.BlockSpec(memory_space=pl.ANY)


def near(*arrays):
    return [pltpu.with_memory_space_constraint(x, pltpu.VMEM) for x in arrays]


def far(*arrays):
    return [pltpu.with_memory_space_constraint(x, pltpu.HBM) for x in arrays]


def params(mib):
    return pltpu.CompilerParams(vmem_limit_bytes=mib << 20)


def start_loads(sources, targets, groups, sems):
    copies = []
    for n, (start, stop) in enumerate(groups):
        rows = pl.ds(start, stop - start)
        pair = [
            pltpu.make_async_copy(source.at[rows], target.at[rows], sems.at[n, k])
            for k, (source, target) in enumerate(zip(sources, targets))
        ]
        for copy in pair:
            copy.start()
        copies.append(pair)
    return copies


def left_kernel(m_hbm, g_hbm, r_hbm, left_ref, m_ref, g_ref, r_ref, both_ref, sum_ref, sems, r_sem):
    first = pltpu.make_async_copy(r_hbm, r_ref, r_sem)
    first.start()
    loads = start_loads((m_hbm, g_hbm), (m_ref, g_ref), DEEP, sems)
    first.wait()
    high, low = split(r_ref[...].T)
    both_ref[:RANK] = high
    both_ref[RANK:] = low
    for n, (start, stop) in enumerate(DEEP):
        for copy in loads[n]:
            copy.wait()
        high, low = split(m_ref[start:stop] + g_ref[start:stop].astype(F32))
        wide = dot(both_ref[:, start:stop], high)
        part = wide[:RANK] + wide[RANK:] + dot(both_ref[:RANK, start:stop], low)
        sum_ref[...] = part if n == 0 else sum_ref[...] + part
    left_ref[...] = sum_ref[...].T


def left_of(m, g, r):
    return pl.pallas_call(
        left_kernel,
        in_specs=[ANY, ANY, ANY],
        out_specs=WHOLE,
        out_shape=pltpu.VMEM((R, RANK), F32),
        scratch_shapes=[
            pltpu.VMEM((C, R), F32),
            pltpu.VMEM((C, R), BF16),
            pltpu.VMEM((C, RANK), F32),
            pltpu.VMEM((2 * RANK, C), BF16),
            pltpu.VMEM((RANK, R), F32),
            pltpu.SemaphoreType.DMA((len(DEEP), 2)),
            pltpu.SemaphoreType.DMA,
        ],
        compiler_params=params(14),
        cost_estimate=pl.CostEstimate(flops=6 * R * C * RANK, bytes_accessed=R * C * 6, transcendentals=0),
        name="left_part",
    )(*far(m, g, r))


def spread_kernel(parts_ref, out_ref, token_ref):
    total = jnp.sum(parts_ref[...], axis=0, keepdims=True)
    out_ref[...] = jnp.broadcast_to(total, out_ref.shape)
    token_ref[...] = total[0, :8]


def sum_and_spread(parts):
    return pl.pallas_call(
        spread_kernel,
        out_shape=[pltpu.VMEM(parts.shape, F32), pltpu.VMEM((8, RANK), F32)],
        in_specs=[WHOLE],
        out_specs=[WHOLE, WHOLE],
        compiler_params=params(4),
        cost_estimate=pl.CostEstimate(flops=parts.size, bytes_accessed=8 * parts.size, transcendentals=0),
        name="sum_and_spread",
    )(*near(parts))


def split_kernel(m_hbm, g_hbm, token_ref, out_ref, m_ref, g_ref, sems):
    loads = start_loads((m_hbm, g_hbm), (m_ref, g_ref), EVEN, sems)
    for n, (start, stop) in enumerate(EVEN):
        for copy in loads[n]:
            copy.wait()
        high, low = split(m_ref[start:stop] + g_ref[start:stop].astype(F32))
        out_ref[start:stop] = high
        out_ref[C + start : C + stop] = low


def split_of(m, g, token):
    return pl.pallas_call(
        split_kernel,
        in_specs=[ANY, ANY, WHOLE],
        out_specs=WHOLE,
        out_shape=pltpu.VMEM((2 * C, R), BF16),
        scratch_shapes=[
            pltpu.VMEM((C, R), F32),
            pltpu.VMEM((C, R), BF16),
            pltpu.SemaphoreType.DMA((len(EVEN), 2)),
        ],
        compiler_params=params(8),
        cost_estimate=pl.CostEstimate(flops=4 * R * C, bytes_accessed=R * C * 10, transcendentals=0),
        name="split_blend",
    )(*far(m, g), *near(token))


def weighted_kernel(core_ref, left_ref, blend_ref, give_ref, keep_ref, both_ref):
    left = left_ref[...]
    high, low = split(left)
    rest = (left - high.astype(F32) - low.astype(F32)).astype(BF16)
    both_ref[:, :RANK] = high
    both_ref[:, RANK:] = low
    wide = dot(high, both_ref[...], ((0,), (0,)))
    mixed = wide[:, RANK:] + dot(high, rest, ((0,), (0,)))
    gram = wide[:, :RANK] + (mixed + mixed.T + dot(low, low, ((0,), (0,))))
    give_ref[HALF:] = gram
    keep_ref[HALF:] = gram
    core = core_ref[0]
    for out_ref, base in ((give_ref, HALF - core * HALF), (keep_ref, core * HALF)):
        for step in range(0, HALF, HALF // 2):
            high = blend_ref[pl.ds(pl.multiple_of(base + step, 16), HALF // 2)]
            low = blend_ref[pl.ds(pl.multiple_of(base + C + step, 16), HALF // 2)]
            wide = dot(high, both_ref[...])
            out_ref[step : step + HALF // 2] = wide[:, :RANK] + wide[:, RANK:] + dot(low, both_ref[:, :RANK])


def weighted_of(core, left, blend):
    return pl.pallas_call(
        weighted_kernel,
        in_specs=[SMEM, WHOLE, WHOLE],
        out_specs=[WHOLE, WHOLE],
        out_shape=[pltpu.VMEM((HALF + RANK, RANK), F32)] * 2,
        scratch_shapes=[pltpu.VMEM((R, 2 * RANK), BF16)],
        compiler_params=params(6),
        cost_estimate=pl.CostEstimate(flops=6 * R * C * RANK, bytes_accessed=R * C * 4, transcendentals=0),
        name="weighted_part",
    )(core, *near(left, blend))


def inverse_kernel(gram_ref, out_ref, work_ref):
    n, b, t = RANK, BLOCK, 8
    row = lax.broadcasted_iota(jnp.int32, (n, n), 0)
    column = lax.broadcasted_iota(jnp.int32, (n, n), 1)
    work_ref[:, :n] = gram_ref[...]
    work_ref[:, n:] = jnp.where(row == column, 1.0, 0.0)
    place = lax.broadcasted_iota(jnp.int32, (t, n), 0)
    for o in range(0, n, b):
        upper = [work_ref[o + k : o + k + t, :n] for k in range(0, b, t)]
        inverse = [work_ref[o + k : o + k + t, n:] for k in range(0, b, t)]
        pivots = []
        for k in range(b // t):
            below = range(k, b // t)
            at = o + k * t
            columns = {q: [jnp.broadcast_to(upper[q][:, at + j : at + j + 1], (t, n)) for j in range(t)] for q in below}
            held = jnp.zeros((t, n), F32)
            for i in range(t):
                pivot = 1.0 / jnp.broadcast_to(columns[k][i][i : i + 1], (t, n))
                held = jnp.where(place == i, pivot, held)
                line = [columns[k][j][i : i + 1] for j in range(t)]
                upper_line, inverse_line = upper[k][i : i + 1], inverse[k][i : i + 1]
                for q in below:
                    factor = columns[q][i] * pivot
                    if q == k:
                        factor = jnp.where(place > i, factor, 0.0)
                    for j in range(i + 1, t):
                        columns[q][j] = columns[q][j] - factor * line[j]
                    upper[q] = upper[q] - factor * upper_line
                    inverse[q] = inverse[q] - factor * inverse_line
            pivots.append(held)
        root = jnp.sqrt(jnp.concatenate(pivots, axis=0))
        upper_block = jnp.concatenate(upper, axis=0) * root
        inverse_block = jnp.concatenate(inverse, axis=0) * root
        out_ref[o : o + b] = inverse_block
        if o + b < n:
            done = jnp.concatenate([upper_block, inverse_block], axis=1)
            work_ref[o + b :] -= dot(upper_block[:, o + b :], done, ((0,), (0,)), HIGH)


def inverse_of(gram):
    return pl.pallas_call(
        inverse_kernel,
        out_shape=pltpu.VMEM((RANK, RANK), F32),
        in_specs=[WHOLE],
        out_specs=WHOLE,
        scratch_shapes=[pltpu.VMEM((RANK, 2 * RANK), F32)],
        compiler_params=params(2),
        cost_estimate=pl.CostEstimate(flops=60 << 30, bytes_accessed=1 << 17, transcendentals=0),
        name="inverse_factor",
    )(*near(gram))


def across_kernel(part_ref, got_ref, inverse_ref, across_ref, colsq_ref):
    high, low = split(inverse_ref[...].T)
    three = jnp.concatenate([high, high, low], axis=0)
    high, low = split(part_ref[...] + got_ref[...])
    across = dot(jnp.concatenate([high, low, high], axis=1), three)
    across_ref[...] = across
    colsq_ref[...] = jnp.broadcast_to(jnp.sum(across * across, axis=0, keepdims=True), colsq_ref.shape)


def across_of(part, got, inverse):
    return pl.pallas_call(
        across_kernel,
        in_specs=[WHOLE, WHOLE, WHOLE],
        out_specs=[WHOLE, WHOLE],
        out_shape=[pltpu.VMEM((HALF, RANK), F32), pltpu.VMEM((64, RANK), F32)],
        compiler_params=params(4),
        cost_estimate=pl.CostEstimate(flops=6 * C * RANK * RANK, bytes_accessed=C * RANK * 8, transcendentals=0),
        name="across_part",
    )(*near(part, got, inverse))


def store(source, target, groups, sems, n):
    rows = pl.ds(groups[n][0], groups[n][1] - groups[n][0])
    copy = pltpu.make_async_copy(source.at[rows], target.at[rows], sems.at[n])
    copy.start()
    return copy


def momentum_kernel(
    core_ref, m_hbm, g_hbm, left_hbm, inverse_ref, mine_ref, other_ref,
    new_hbm, basis_ref, across_ref, m_ref, g_ref, left_ref, new_ref, sems, left_sem, out_sems,
):
    load = pltpu.make_async_copy(left_hbm, left_ref, left_sem)
    load.start()
    loads = start_loads((m_hbm, g_hbm), (m_ref, g_ref), EVEN, sems)
    high, low = split(inverse_ref[...])
    load.wait()
    both = split(left_ref[...])
    basis = dot(jnp.concatenate([high, high], axis=1), jnp.concatenate(both, axis=1), ((1,), (1,)))
    high, low = split(basis + dot(low, both[0], ((1,), (1,))))
    basis_ref[:RANK] = high
    basis_ref[RANK : 2 * RANK] = high
    basis_ref[2 * RANK :] = low
    mine = core_ref[0] * HALF
    across_ref[pl.ds(pl.multiple_of(mine, 8), HALF)] = mine_ref[...]
    across_ref[pl.ds(pl.multiple_of(HALF - mine, 8), HALF)] = other_ref[...]
    stores = []
    for n, (start, stop) in enumerate(EVEN):
        for copy in loads[n]:
            copy.wait()
        wide = jnp.concatenate(split(across_ref[start:stop] * 0.05), axis=1)
        blend = m_ref[start:stop] + g_ref[start:stop].astype(F32)
        new_ref[start:stop] = blend - dot(wide, basis_ref[: 2 * RANK])
        stores.append(store(new_ref, new_hbm, EVEN, out_sems, n))
    for copy in stores:
        copy.wait()


def momentum_of(core, m, g, left, inverse, mine, other):
    return pl.pallas_call(
        momentum_kernel,
        in_specs=[SMEM, ANY, ANY, ANY, WHOLE, WHOLE, WHOLE],
        out_specs=[ANY, WHOLE, WHOLE],
        out_shape=[pltpu.HBM((C, R), F32), pltpu.VMEM((3 * RANK, R), BF16), pltpu.VMEM((C, RANK), F32)],
        scratch_shapes=[
            pltpu.VMEM((C, R), F32),
            pltpu.VMEM((C, R), BF16),
            pltpu.VMEM((R, RANK), F32),
            pltpu.VMEM((C, R), F32),
            pltpu.SemaphoreType.DMA((len(EVEN), 2)),
            pltpu.SemaphoreType.DMA,
            pltpu.SemaphoreType.DMA((len(EVEN),)),
        ],
        compiler_params=params(14),
        cost_estimate=pl.CostEstimate(flops=4 * R * C * RANK, bytes_accessed=R * C * 10, transcendentals=0),
        name="new_momentum",
    )(core, *far(m, g), left, *near(inverse, mine, other))


def update_kernel(across_ref, colsq_ref, basis_ref, update_hbm, update_ref, sems):
    colsq = jnp.sum(colsq_ref[...], axis=0, keepdims=True)
    scale = (ROWS * COLS / RANK) ** 0.5 / jnp.sqrt(colsq + 1e-06)
    stores = []
    for n, (start, stop) in enumerate(EVEN):
        high, low = split(across_ref[start:stop] * scale)
        product = dot(jnp.concatenate([high, low, high], axis=1), basis_ref[...])
        update_ref[start:stop] = product.astype(BF16)
        stores.append(store(update_ref, update_hbm, EVEN, sems, n))
    for copy in stores:
        copy.wait()


def update_of(across, colsq, basis):
    return pl.pallas_call(
        update_kernel,
        in_specs=[WHOLE, WHOLE, WHOLE],
        out_specs=ANY,
        out_shape=pltpu.HBM((C, R), BF16),
        scratch_shapes=[pltpu.VMEM((C, R), BF16), pltpu.SemaphoreType.DMA((len(EVEN),))],
        compiler_params=params(6),
        cost_estimate=pl.CostEstimate(flops=6 * R * C * RANK, bytes_accessed=R * C * 2, transcendentals=0),
        name="update",
    )(*near(across, colsq, basis))


def exchange(blocks, axes):
    return lax.all_to_all(blocks, axes, 0, 0)


def swap_core(block):
    return lax.ppermute(block, "core", [(0, 1), (1, 0)])


def swap_y(block, step):
    pairs = [(i, i ^ 2 if i % 2 == step else 7 - (i ^ 1)) for i in range(8)]
    return lax.ppermute(block, ("y", "core"), pairs)


def body(momentum, gradient, right_factor):
    m, g = momentum.T, gradient.T
    core = lax.axis_index("core").astype(jnp.int32).reshape(1)
    partial = left_of(m, g, right_factor)
    spread, token = sum_and_spread(exchange(partial.reshape(32, R // 32, RANK), ("x", "z")))
    left = exchange(spread, ("x", "z")).reshape(R, RANK)
    blend = split_of(m, g, token)

    give, part = weighted_of(core, left, blend)
    part = part + swap_core(give)
    part = part + swap_y(part, 0)
    part, gram = part[:HALF], part[HALF:]
    inverse = inverse_of(gram + swap_y(gram, 1))
    mine, colsq = across_of(part, swap_y(part, 1), inverse)

    colsq = exchange(colsq.reshape(64, 1, RANK), ("core", "x", "z")).reshape(64, RANK)
    new_momentum, basis, across = momentum_of(core, m, g, left, inverse, mine, swap_core(mine))
    update = update_of(across, colsq, basis)
    return (new_momentum.T, update.T)


def solution(mesh):
    own = jax.sharding.Mesh(mesh.devices.reshape(4, 2, 4, 8), ("y", "core", "x", "z"))
    whole = P(("y", "core"), ("x", "z"))
    return jax.shard_map(
        body, mesh=own, in_specs=(whole, whole, P(("x", "z"), None)), out_specs=(whole, whole), check_vma=False
    )
```

```python
import jax
import jax.numpy as jnp
from jax import lax
from jax.experimental import pallas as pl
from jax.experimental.pallas import tpu as pltpu
from jax.sharding import PartitionSpec as P

ROWS = 8192
COLS = 26624
RANK = 128
HIGH = lax.Precision.HIGHEST
F32 = jnp.float32
BF16 = jnp.bfloat16

C = 832
R = 1024
DEEP = ((0, 320), (320, 832))
EVEN = tuple((n, n + 208) for n in range(0, C, 208))
BLOCK = 64

HALF = C // 2
SMEM = pl.BlockSpec(memory_space=pltpu.SMEM)


def dot(first, second, dims=((1,), (0,)), precision=None):
    return lax.dot_general(first, second, (dims, ((), ())), precision=precision, preferred_element_type=F32)


def split(x):
    high = x.astype(BF16)
    return high, (x - high.astype(F32)).astype(BF16)


WHOLE = pl.BlockSpec(memory_space=pltpu.VMEM)
ANY = pl.BlockSpec(memory_space=pl.ANY)


def near(*arrays):
    return [pltpu.with_memory_space_constraint(x, pltpu.VMEM) for x in arrays]


def far(*arrays):
    return [pltpu.with_memory_space_constraint(x, pltpu.HBM) for x in arrays]


def params(mib):
    return pltpu.CompilerParams(vmem_limit_bytes=mib << 20)


def start_loads(sources, targets, groups, sems):
    copies = []
    for n, (start, stop) in enumerate(groups):
        rows = pl.ds(start, stop - start)
        pair = [
            pltpu.make_async_copy(source.at[rows], target.at[rows], sems.at[n, k])
            for k, (source, target) in enumerate(zip(sources, targets))
        ]
        for copy in pair:
            copy.start()
        copies.append(pair)
    return copies


def left_kernel(core_ref, m_hbm, g_hbm, r_hbm, left_ref, m_ref, g_ref, r_ref, both_ref, sum_ref, sems, r_sem):
    first = pltpu.make_async_copy(r_hbm, r_ref, r_sem)
    first.start()
    loads = start_loads((m_hbm, g_hbm), (m_ref, g_ref), DEEP, sems)
    first.wait()
    high, low = split(r_ref[...].T)
    both_ref[:RANK] = high
    both_ref[RANK:] = low
    for n, (start, stop) in enumerate(DEEP):
        for copy in loads[n]:
            copy.wait()
        high, low = split(m_ref[start:stop] + g_ref[start:stop].astype(F32))
        wide = dot(both_ref[:, start:stop], high)
        part = wide[:RANK] + wide[RANK:] + dot(both_ref[:RANK, start:stop], low)
        sum_ref[...] = part if n == 0 else sum_ref[...] + part
    left_ref[...] = sum_ref[...].T


def left_of(core, m, g, r):
    return pl.pallas_call(
        left_kernel,
        in_specs=[SMEM, ANY, ANY, ANY],
        out_specs=WHOLE,
        out_shape=pltpu.VMEM((R, RANK), F32),
        scratch_shapes=[
            pltpu.VMEM((C, R), F32),
            pltpu.VMEM((C, R), BF16),
            pltpu.VMEM((C, RANK), F32),
            pltpu.VMEM((2 * RANK, C), BF16),
            pltpu.VMEM((RANK, R), F32),
            pltpu.SemaphoreType.DMA((len(DEEP), 2)),
            pltpu.SemaphoreType.DMA,
        ],
        compiler_params=params(14),
        cost_estimate=pl.CostEstimate(flops=6 * R * C * RANK, bytes_accessed=R * C * 6, transcendentals=0),
        name="left_part",
    )(core, *far(m, g, r))


def spread_kernel(parts_ref, out_ref):
    out_ref[...] = jnp.broadcast_to(jnp.sum(parts_ref[...], axis=0, keepdims=True), out_ref.shape)


def sum_and_spread(parts, count):
    return pl.pallas_call(
        spread_kernel,
        out_shape=pltpu.VMEM((count,) + parts.shape[1:], F32),
        in_specs=[WHOLE],
        out_specs=WHOLE,
        compiler_params=params(4),
        cost_estimate=pl.CostEstimate(flops=parts.size, bytes_accessed=8 * parts.size, transcendentals=0),
        name="sum_and_spread",
    )(*near(parts))


def weighted_kernel(core_ref, left_ref, m_ref, g_ref, give_ref, keep_ref, both_ref):
    core = core_ref[0]
    step = HALF // 2
    left = left_ref[...]
    high, low = split(left)
    rest = (left - high.astype(F32) - low.astype(F32)).astype(BF16)
    both_ref[:, :RANK] = high
    both_ref[:, RANK:] = low
    wide = dot(high, both_ref[...], ((0,), (0,)))
    mixed = wide[:, RANK:] + dot(high, rest, ((0,), (0,)))
    gram = wide[:, :RANK] + (mixed + mixed.T + dot(low, low, ((0,), (0,))))
    give_ref[HALF:] = gram
    keep_ref[HALF:] = gram
    theirs, mine = HALF - core * HALF, core * HALF
    for out_ref, base, start in (
        (give_ref, theirs, 0),
        (give_ref, theirs, step),
        (keep_ref, mine, 0),
        (keep_ref, mine, step),
    ):
        rows = pl.ds(pl.multiple_of(base + start, 16), step)
        high, low = split(m_ref[rows] + g_ref[rows].astype(F32))
        wide = dot(high, both_ref[...])
        out_ref[start : start + step] = wide[:, :RANK] + wide[:, RANK:] + dot(low, both_ref[:, :RANK])


def weighted_of(core, left, m, g):
    return pl.pallas_call(
        weighted_kernel,
        in_specs=[SMEM, WHOLE, WHOLE, WHOLE],
        out_specs=[WHOLE, WHOLE],
        out_shape=[pltpu.VMEM((HALF + RANK, RANK), F32)] * 2,
        scratch_shapes=[
            pltpu.VMEM((R, 2 * RANK), BF16),
        ],
        compiler_params=params(8),
        cost_estimate=pl.CostEstimate(flops=6 * R * C * RANK, bytes_accessed=R * C * 6, transcendentals=0),
        name="weighted_part",
    )(core, *near(left, m, g))


def inverse_kernel(gram_ref, out_ref, work_ref):
    n, b, t = RANK, BLOCK, 8
    row = lax.broadcasted_iota(jnp.int32, (n, n), 0)
    column = lax.broadcasted_iota(jnp.int32, (n, n), 1)
    work_ref[:, :n] = gram_ref[...]
    work_ref[:, n:] = jnp.where(row == column, 1.0, 0.0)
    place = lax.broadcasted_iota(jnp.int32, (t, n), 0)
    for o in range(0, n, b):
        upper = [work_ref[o + k : o + k + t, :n] for k in range(0, b, t)]
        inverse = [work_ref[o + k : o + k + t, n:] for k in range(0, b, t)]
        pivots = []
        for k in range(b // t):
            below = range(k, b // t)
            at = o + k * t
            columns = {q: [jnp.broadcast_to(upper[q][:, at + j : at + j + 1], (t, n)) for j in range(t)] for q in below}
            held = jnp.zeros((t, n), F32)
            for i in range(t):
                pivot = 1.0 / jnp.broadcast_to(columns[k][i][i : i + 1], (t, n))
                held = jnp.where(place == i, pivot, held)
                line = [columns[k][j][i : i + 1] for j in range(t)]
                upper_line, inverse_line = upper[k][i : i + 1], inverse[k][i : i + 1]
                for q in below:
                    factor = columns[q][i] * pivot
                    if q == k:
                        factor = jnp.where(place > i, factor, 0.0)
                    for j in range(i + 1, t):
                        columns[q][j] = columns[q][j] - factor * line[j]
                    upper[q] = upper[q] - factor * upper_line
                    inverse[q] = inverse[q] - factor * inverse_line
            pivots.append(held)
        root = jnp.sqrt(jnp.concatenate(pivots, axis=0))
        upper_block = jnp.concatenate(upper, axis=0) * root
        inverse_block = jnp.concatenate(inverse, axis=0) * root
        out_ref[o : o + b] = inverse_block
        if o + b < n:
            done = jnp.concatenate([upper_block, inverse_block], axis=1)
            work_ref[o + b :] -= dot(upper_block[:, o + b :], done, ((0,), (0,)), HIGH)


def inverse_of(gram):
    return pl.pallas_call(
        inverse_kernel,
        out_shape=pltpu.VMEM((RANK, RANK), F32),
        in_specs=[WHOLE],
        out_specs=WHOLE,
        scratch_shapes=[pltpu.VMEM((RANK, 2 * RANK), F32)],
        compiler_params=params(2),
        cost_estimate=pl.CostEstimate(flops=60 << 30, bytes_accessed=1 << 17, transcendentals=0),
        name="inverse_factor",
    )(*near(gram))


def across_kernel(part_ref, got_ref, inverse_ref, across_ref, colsq_ref):
    high, low = split(inverse_ref[...].T)
    three = jnp.concatenate([high, high, low], axis=0)
    high, low = split(part_ref[...] + got_ref[...])
    across = dot(jnp.concatenate([high, low, high], axis=1), three)
    across_ref[...] = across
    colsq_ref[...] = jnp.broadcast_to(jnp.sum(across * across, axis=0, keepdims=True), colsq_ref.shape)


def across_of(part, got, inverse):
    return pl.pallas_call(
        across_kernel,
        in_specs=[WHOLE, WHOLE, WHOLE],
        out_specs=[WHOLE, WHOLE],
        out_shape=[pltpu.VMEM((HALF, RANK), F32), pltpu.VMEM((64, RANK), F32)],
        compiler_params=params(4),
        cost_estimate=pl.CostEstimate(flops=6 * C * RANK * RANK, bytes_accessed=C * RANK * 8, transcendentals=0),
        name="across_part",
    )(*near(part, got, inverse))


def store(source, target, groups, sems, n):
    rows = pl.ds(groups[n][0], groups[n][1] - groups[n][0])
    copy = pltpu.make_async_copy(source.at[rows], target.at[rows], sems.at[n])
    copy.start()
    return copy


def momentum_kernel(
    core_ref, m_hbm, g_hbm, left_hbm, inverse_ref, mine_ref, other_ref,
    new_hbm, basis_ref, across_ref, m_ref, g_ref, left_ref, new_ref, sems, left_sem, out_sems,
):
    load = pltpu.make_async_copy(left_hbm, left_ref, left_sem)
    load.start()
    loads = start_loads((m_hbm, g_hbm), (m_ref, g_ref), EVEN, sems)
    high, low = split(inverse_ref[...])
    load.wait()
    both = split(left_ref[...])
    basis = dot(jnp.concatenate([high, high], axis=1), jnp.concatenate(both, axis=1), ((1,), (1,)))
    high, low = split(basis + dot(low, both[0], ((1,), (1,))))
    basis_ref[:RANK] = high
    basis_ref[RANK : 2 * RANK] = high
    basis_ref[2 * RANK :] = low
    mine = core_ref[0] * HALF
    across_ref[pl.ds(pl.multiple_of(mine, 8), HALF)] = mine_ref[...]
    across_ref[pl.ds(pl.multiple_of(HALF - mine, 8), HALF)] = other_ref[...]
    stores = []
    for n, (start, stop) in enumerate(EVEN):
        for copy in loads[n]:
            copy.wait()
        wide = jnp.concatenate(split(across_ref[start:stop] * 0.05), axis=1)
        blend = m_ref[start:stop] + g_ref[start:stop].astype(F32)
        new_ref[start:stop] = blend - dot(wide, basis_ref[: 2 * RANK])
        stores.append(store(new_ref, new_hbm, EVEN, out_sems, n))
    for copy in stores:
        copy.wait()


def momentum_of(core, m, g, left, inverse, mine, other):
    return pl.pallas_call(
        momentum_kernel,
        in_specs=[SMEM, ANY, ANY, ANY, WHOLE, WHOLE, WHOLE],
        out_specs=[ANY, WHOLE, WHOLE],
        out_shape=[pltpu.HBM((C, R), F32), pltpu.VMEM((3 * RANK, R), BF16), pltpu.VMEM((C, RANK), F32)],
        scratch_shapes=[
            pltpu.VMEM((C, R), F32),
            pltpu.VMEM((C, R), BF16),
            pltpu.VMEM((R, RANK), F32),
            pltpu.VMEM((C, R), F32),
            pltpu.SemaphoreType.DMA((len(EVEN), 2)),
            pltpu.SemaphoreType.DMA,
            pltpu.SemaphoreType.DMA((len(EVEN),)),
        ],
        compiler_params=params(14),
        cost_estimate=pl.CostEstimate(flops=4 * R * C * RANK, bytes_accessed=R * C * 10, transcendentals=0),
        name="new_momentum",
    )(core, *far(m, g), left, *near(inverse, mine, other))


def update_kernel(across_ref, colsq_ref, basis_ref, update_hbm, update_ref, sems):
    colsq = jnp.sum(colsq_ref[...], axis=0, keepdims=True)
    scale = (ROWS * COLS / RANK) ** 0.5 / jnp.sqrt(colsq + 1e-06)
    stores = []
    for n, (start, stop) in enumerate(EVEN):
        high, low = split(across_ref[start:stop] * scale)
        product = dot(jnp.concatenate([high, low, high], axis=1), basis_ref[...])
        update_ref[start:stop] = product.astype(BF16)
        stores.append(store(update_ref, update_hbm, EVEN, sems, n))
    for copy in stores:
        copy.wait()


def update_of(across, colsq, basis):
    return pl.pallas_call(
        update_kernel,
        in_specs=[WHOLE, WHOLE, WHOLE],
        out_specs=ANY,
        out_shape=pltpu.HBM((C, R), BF16),
        scratch_shapes=[pltpu.VMEM((C, R), BF16), pltpu.SemaphoreType.DMA((len(EVEN),))],
        compiler_params=params(6),
        cost_estimate=pl.CostEstimate(flops=6 * R * C * RANK, bytes_accessed=R * C * 2, transcendentals=0),
        name="update",
    )(*near(across, colsq, basis))


def exchange(blocks, axes):
    return lax.all_to_all(blocks, axes, 0, 0)


def swap_core(block):
    return lax.ppermute(block, "core", [(0, 1), (1, 0)])


def swap_y(block, step):
    pairs = [(i, i ^ 2 if i % 2 == step else 7 - (i ^ 1)) for i in range(8)]
    return lax.ppermute(block, ("y", "core"), pairs)


def body(momentum, gradient, right_factor):
    m, g = momentum.T, gradient.T
    core = lax.axis_index("core").astype(jnp.int32).reshape(1)
    partial = left_of(core, m, g, right_factor)
    quarter = sum_and_spread(exchange(partial.reshape(4, R // 4, RANK), "x"), 1)
    spread = sum_and_spread(exchange(quarter.reshape(8, R // 32, RANK), "z"), 32)
    left = exchange(spread, ("x", "z")).reshape(R, RANK)

    give, part = weighted_of(core, left, m, g)
    part = part + swap_core(give)
    part = part + swap_y(part, 0)
    part, gram = part[:HALF], part[HALF:]
    inverse = inverse_of(gram + swap_y(gram, 1))
    mine, colsq = across_of(part, swap_y(part, 1), inverse)

    colsq = exchange(colsq.reshape(64, 1, RANK), ("core", "x", "z")).reshape(64, RANK)
    new_momentum, basis, across = momentum_of(core, m, g, left, inverse, mine, swap_core(mine))
    update = update_of(across, colsq, basis)
    return (new_momentum.T, update.T)


def solution(mesh):
    own = jax.sharding.Mesh(mesh.devices.reshape(4, 2, 4, 8), ("y", "core", "x", "z"))
    whole = P(("y", "core"), ("x", "z"))
    return jax.shard_map(
        body, mesh=own, in_specs=(whole, whole, P(("x", "z"), None)), out_specs=(whole, whole), check_vma=False
    )
```

```python
import jax
import jax.numpy as jnp
from jax import lax
from jax.experimental import pallas as pl
from jax.experimental.pallas import tpu as pltpu
from jax.sharding import PartitionSpec as P

ROWS = 8192
COLS = 26624
RANK = 128
HIGH = lax.Precision.HIGHEST
F32 = jnp.float32
BF16 = jnp.bfloat16

C = 832
R = 1024
DEEP = ((0, 320), (320, 832))
EVEN = tuple((n, n + 208) for n in range(0, C, 208))
BLOCK = 64

HALF = C // 2
SMEM = pl.BlockSpec(memory_space=pltpu.SMEM)


def dot(first, second, dims=((1,), (0,)), precision=None):
    return lax.dot_general(first, second, (dims, ((), ())), precision=precision, preferred_element_type=F32)


def split(x):
    high = x.astype(BF16)
    return high, (x - high.astype(F32)).astype(BF16)


WHOLE = pl.BlockSpec(memory_space=pltpu.VMEM)
ANY = pl.BlockSpec(memory_space=pl.ANY)


def near(*arrays):
    return [pltpu.with_memory_space_constraint(x, pltpu.VMEM) for x in arrays]


def far(*arrays):
    return [pltpu.with_memory_space_constraint(x, pltpu.HBM) for x in arrays]


def params(mib):
    return pltpu.CompilerParams(vmem_limit_bytes=mib << 20)


def start_loads(sources, targets, groups, sems):
    copies = []
    for n, (start, stop) in enumerate(groups):
        rows = pl.ds(start, stop - start)
        pair = [
            pltpu.make_async_copy(source.at[rows], target.at[rows], sems.at[n, k])
            for k, (source, target) in enumerate(zip(sources, targets))
        ]
        for copy in pair:
            copy.start()
        copies.append(pair)
    return copies


def left_kernel(core_ref, m_hbm, g_hbm, r_hbm, left_ref, m_ref, g_ref, r_ref, both_ref, sum_ref, sems, r_sem):
    first = pltpu.make_async_copy(r_hbm, r_ref, r_sem)
    first.start()
    loads = start_loads((m_hbm, g_hbm), (m_ref, g_ref), DEEP, sems)
    first.wait()
    high, low = split(r_ref[...].T)
    both_ref[:RANK] = high
    both_ref[RANK:] = low
    for n, (start, stop) in enumerate(DEEP):
        for copy in loads[n]:
            copy.wait()
        high, low = split(m_ref[start:stop] + g_ref[start:stop].astype(F32))
        wide = dot(both_ref[:, start:stop], high)
        part = wide[:RANK] + wide[RANK:] + dot(both_ref[:RANK, start:stop], low)
        sum_ref[...] = part if n == 0 else sum_ref[...] + part
    left_ref[...] = sum_ref[...].T


def left_of(core, m, g, r):
    return pl.pallas_call(
        left_kernel,
        in_specs=[SMEM, ANY, ANY, ANY],
        out_specs=WHOLE,
        out_shape=pltpu.VMEM((R, RANK), F32),
        scratch_shapes=[
            pltpu.VMEM((C, R), F32),
            pltpu.VMEM((C, R), BF16),
            pltpu.VMEM((C, RANK), F32),
            pltpu.VMEM((2 * RANK, C), BF16),
            pltpu.VMEM((RANK, R), F32),
            pltpu.SemaphoreType.DMA((len(DEEP), 2)),
            pltpu.SemaphoreType.DMA,
        ],
        compiler_params=params(14),
        cost_estimate=pl.CostEstimate(flops=6 * R * C * RANK, bytes_accessed=R * C * 6, transcendentals=0),
        name="left_part",
    )(core, *far(m, g, r))


def spread_kernel(parts_ref, out_ref):
    out_ref[...] = jnp.broadcast_to(jnp.sum(parts_ref[...], axis=0, keepdims=True), out_ref.shape)


def sum_and_spread(parts, count):
    return pl.pallas_call(
        spread_kernel,
        out_shape=pltpu.VMEM((count,) + parts.shape[1:], F32),
        in_specs=[WHOLE],
        out_specs=WHOLE,
        compiler_params=params(4),
        cost_estimate=pl.CostEstimate(flops=parts.size, bytes_accessed=8 * parts.size, transcendentals=0),
        name="sum_and_spread",
    )(*near(parts))


def product(core_ref, away, both_ref, m_ref, g_ref, out_ref):
    base = (1 - core_ref[0] if away else core_ref[0]) * HALF
    for start in range(0, HALF, HALF // 2):
        rows = pl.ds(pl.multiple_of(base + start, 16), HALF // 2)
        high, low = split(m_ref[rows] + g_ref[rows].astype(F32))
        wide = dot(high, both_ref[...])
        out_ref[start : start + HALF // 2] = wide[:, :RANK] + wide[:, RANK:] + dot(low, both_ref[:, :RANK])


def give_kernel(core_ref, left_ref, m_ref, g_ref, give_ref, both_ref):
    left = left_ref[...]
    high, low = split(left)
    rest = (left - high.astype(F32) - low.astype(F32)).astype(BF16)
    both_ref[:, :RANK] = high
    both_ref[:, RANK:] = low
    wide = dot(high, both_ref[...], ((0,), (0,)))
    mixed = wide[:, RANK:] + dot(high, rest, ((0,), (0,)))
    give_ref[HALF:] = wide[:, :RANK] + (mixed + mixed.T + dot(low, low, ((0,), (0,))))
    product(core_ref, True, both_ref, m_ref, g_ref, give_ref)


def keep_kernel(core_ref, both_ref, m_ref, g_ref, give_ref, keep_ref):
    product(core_ref, False, both_ref, m_ref, g_ref, keep_ref)
    keep_ref[HALF:] = give_ref[HALF:]


def weighted_of(core, left, m, g):
    out = pltpu.VMEM((HALF + RANK, RANK), F32)
    cost = pl.CostEstimate(flops=3 * R * C * RANK, bytes_accessed=R * C * 3, transcendentals=0)
    give, both = pl.pallas_call(
        give_kernel,
        in_specs=[SMEM, WHOLE, WHOLE, WHOLE],
        out_specs=[WHOLE, WHOLE],
        out_shape=[out, pltpu.VMEM((R, 2 * RANK), BF16)],
        compiler_params=params(8),
        cost_estimate=cost,
        name="weighted_give",
    )(core, *near(left, m, g))
    keep = pl.pallas_call(
        keep_kernel,
        in_specs=[SMEM, WHOLE, WHOLE, WHOLE, WHOLE],
        out_specs=WHOLE,
        out_shape=out,
        compiler_params=params(8),
        cost_estimate=cost,
        name="weighted_keep",
    )(core, *near(both, m, g, give))
    return give, keep


def inverse_kernel(gram_ref, got_ref, out_ref, work_ref):
    n, b, t = RANK, BLOCK, 8
    row = lax.broadcasted_iota(jnp.int32, (n, n), 0)
    column = lax.broadcasted_iota(jnp.int32, (n, n), 1)
    work_ref[:, :n] = gram_ref[...] + got_ref[...]
    work_ref[:, n:] = jnp.where(row == column, 1.0, 0.0)
    place = lax.broadcasted_iota(jnp.int32, (t, n), 0)
    for o in range(0, n, b):
        upper = [work_ref[o + k : o + k + t, :n] for k in range(0, b, t)]
        inverse = [work_ref[o + k : o + k + t, n:] for k in range(0, b, t)]
        pivots = []
        for k in range(b // t):
            below = range(k, b // t)
            at = o + k * t
            columns = {q: [jnp.broadcast_to(upper[q][:, at + j : at + j + 1], (t, n)) for j in range(t)] for q in below}
            held = jnp.zeros((t, n), F32)
            for i in range(t):
                pivot = 1.0 / jnp.broadcast_to(columns[k][i][i : i + 1], (t, n))
                held = jnp.where(place == i, pivot, held)
                line = [columns[k][j][i : i + 1] for j in range(t)]
                upper_line, inverse_line = upper[k][i : i + 1], inverse[k][i : i + 1]
                for q in below:
                    factor = columns[q][i] * pivot
                    if q == k:
                        factor = jnp.where(place > i, factor, 0.0)
                    for j in range(i + 1, t):
                        columns[q][j] = columns[q][j] - factor * line[j]
                    upper[q] = upper[q] - factor * upper_line
                    inverse[q] = inverse[q] - factor * inverse_line
            pivots.append(held)
        root = jnp.sqrt(jnp.concatenate(pivots, axis=0))
        upper_block = jnp.concatenate(upper, axis=0) * root
        inverse_block = jnp.concatenate(inverse, axis=0) * root
        out_ref[o : o + b] = inverse_block
        if o + b < n:
            done = jnp.concatenate([upper_block, inverse_block], axis=1)
            work_ref[o + b :] -= dot(upper_block[:, o + b :], done, ((0,), (0,)), HIGH)


def inverse_of(gram, got):
    return pl.pallas_call(
        inverse_kernel,
        out_shape=pltpu.VMEM((RANK, RANK), F32),
        in_specs=[WHOLE, WHOLE],
        out_specs=WHOLE,
        scratch_shapes=[pltpu.VMEM((RANK, 2 * RANK), F32)],
        compiler_params=params(2),
        cost_estimate=pl.CostEstimate(flops=60 << 30, bytes_accessed=1 << 17, transcendentals=0),
        name="inverse_factor",
    )(*near(gram, got))


def across_kernel(part_ref, got_ref, inverse_ref, across_ref, colsq_ref):
    high, low = split(inverse_ref[...].T)
    three = jnp.concatenate([high, high, low], axis=0)
    high, low = split(part_ref[...] + got_ref[...])
    across = dot(jnp.concatenate([high, low, high], axis=1), three)
    across_ref[...] = across
    colsq_ref[...] = jnp.broadcast_to(jnp.sum(across * across, axis=0, keepdims=True), colsq_ref.shape)


def across_of(part, got, inverse):
    return pl.pallas_call(
        across_kernel,
        in_specs=[WHOLE, WHOLE, WHOLE],
        out_specs=[WHOLE, WHOLE],
        out_shape=[pltpu.VMEM((HALF, RANK), F32), pltpu.VMEM((64, RANK), F32)],
        compiler_params=params(4),
        cost_estimate=pl.CostEstimate(flops=6 * C * RANK * RANK, bytes_accessed=C * RANK * 8, transcendentals=0),
        name="across_part",
    )(*near(part, got, inverse))


def store(source, target, groups, sems, n):
    rows = pl.ds(groups[n][0], groups[n][1] - groups[n][0])
    copy = pltpu.make_async_copy(source.at[rows], target.at[rows], sems.at[n])
    copy.start()
    return copy


def momentum_kernel(
    core_ref, m_hbm, g_hbm, left_hbm, inverse_ref, mine_ref, other_ref,
    new_hbm, basis_ref, across_ref, m_ref, g_ref, left_ref, new_ref, sems, left_sem, out_sems,
):
    load = pltpu.make_async_copy(left_hbm, left_ref, left_sem)
    load.start()
    loads = start_loads((m_hbm, g_hbm), (m_ref, g_ref), EVEN, sems)
    high, low = split(inverse_ref[...])
    load.wait()
    both = split(left_ref[...])
    basis = dot(jnp.concatenate([high, high], axis=1), jnp.concatenate(both, axis=1), ((1,), (1,)))
    high, low = split(basis + dot(low, both[0], ((1,), (1,))))
    basis_ref[:RANK] = high
    basis_ref[RANK : 2 * RANK] = high
    basis_ref[2 * RANK :] = low
    mine = core_ref[0] * HALF
    across_ref[pl.ds(pl.multiple_of(mine, 8), HALF)] = mine_ref[...]
    across_ref[pl.ds(pl.multiple_of(HALF - mine, 8), HALF)] = other_ref[...]
    stores = []
    for n, (start, stop) in enumerate(EVEN):
        for copy in loads[n]:
            copy.wait()
        wide = jnp.concatenate(split(across_ref[start:stop] * 0.05), axis=1)
        blend = m_ref[start:stop] + g_ref[start:stop].astype(F32)
        new_ref[start:stop] = blend - dot(wide, basis_ref[: 2 * RANK])
        stores.append(store(new_ref, new_hbm, EVEN, out_sems, n))
    for copy in stores:
        copy.wait()


def momentum_of(core, m, g, left, inverse, mine, other):
    return pl.pallas_call(
        momentum_kernel,
        in_specs=[SMEM, ANY, ANY, ANY, WHOLE, WHOLE, WHOLE],
        out_specs=[ANY, WHOLE, WHOLE],
        out_shape=[pltpu.HBM((C, R), F32), pltpu.VMEM((3 * RANK, R), BF16), pltpu.VMEM((C, RANK), F32)],
        scratch_shapes=[
            pltpu.VMEM((C, R), F32),
            pltpu.VMEM((C, R), BF16),
            pltpu.VMEM((R, RANK), F32),
            pltpu.VMEM((C, R), F32),
            pltpu.SemaphoreType.DMA((len(EVEN), 2)),
            pltpu.SemaphoreType.DMA,
            pltpu.SemaphoreType.DMA((len(EVEN),)),
        ],
        compiler_params=params(14),
        cost_estimate=pl.CostEstimate(flops=4 * R * C * RANK, bytes_accessed=R * C * 10, transcendentals=0),
        name="new_momentum",
    )(core, *far(m, g), left, *near(inverse, mine, other))


def update_kernel(across_ref, colsq_ref, basis_ref, update_hbm, update_ref, sems):
    colsq = jnp.sum(colsq_ref[...], axis=0, keepdims=True)
    scale = (ROWS * COLS / RANK) ** 0.5 / jnp.sqrt(colsq + 1e-06)
    stores = []
    for n, (start, stop) in enumerate(EVEN):
        high, low = split(across_ref[start:stop] * scale)
        product = dot(jnp.concatenate([high, low, high], axis=1), basis_ref[...])
        update_ref[start:stop] = product.astype(BF16)
        stores.append(store(update_ref, update_hbm, EVEN, sems, n))
    for copy in stores:
        copy.wait()


def update_of(across, colsq, basis):
    return pl.pallas_call(
        update_kernel,
        in_specs=[WHOLE, WHOLE, WHOLE],
        out_specs=ANY,
        out_shape=pltpu.HBM((C, R), BF16),
        scratch_shapes=[pltpu.VMEM((C, R), BF16), pltpu.SemaphoreType.DMA((len(EVEN),))],
        compiler_params=params(6),
        cost_estimate=pl.CostEstimate(flops=6 * R * C * RANK, bytes_accessed=R * C * 2, transcendentals=0),
        name="update",
    )(*near(across, colsq, basis))


def exchange(blocks, axes):
    return lax.all_to_all(blocks, axes, 0, 0)


def swap_core(block):
    return lax.ppermute(block, "core", [(0, 1), (1, 0)])


def swap_y(block, step):
    pairs = [(i, i ^ 2 if i % 2 == step else 7 - (i ^ 1)) for i in range(8)]
    return lax.ppermute(block, ("y", "core"), pairs)


def body(momentum, gradient, right_factor):
    m, g = momentum.T, gradient.T
    core = lax.axis_index("core").astype(jnp.int32).reshape(1)
    partial = left_of(core, m, g, right_factor)
    quarter = sum_and_spread(exchange(partial.reshape(4, R // 4, RANK), "x"), 1)
    spread = sum_and_spread(exchange(quarter.reshape(8, R // 32, RANK), "z"), 32)
    left = exchange(spread, ("x", "z")).reshape(R, RANK)

    give, part = weighted_of(core, left, m, g)
    part = part + swap_core(give)
    part, gram = part[:HALF], part[HALF:]
    gram = gram + swap_y(gram, 0)
    inverse = inverse_of(gram, swap_y(gram, 1))
    part = part + swap_y(part, 0)
    mine, colsq = across_of(part, swap_y(part, 1), inverse)

    colsq = exchange(colsq.reshape(64, 1, RANK), ("core", "x", "z")).reshape(64, RANK)
    new_momentum, basis, across = momentum_of(core, m, g, left, inverse, mine, swap_core(mine))
    update = update_of(across, colsq, basis)
    return (new_momentum.T, update.T)


def solution(mesh):
    own = jax.sharding.Mesh(mesh.devices.reshape(4, 2, 4, 8), ("y", "core", "x", "z"))
    whole = P(("y", "core"), ("x", "z"))
    return jax.shard_map(
        body, mesh=own, in_specs=(whole, whole, P(("x", "z"), None)), out_specs=(whole, whole), check_vma=False
    )
```

```python
import jax
import jax.numpy as jnp
from jax import lax
from jax.experimental import pallas as pl
from jax.experimental.pallas import tpu as pltpu
from jax.sharding import PartitionSpec as P

ROWS = 8192
COLS = 26624
RANK = 128
HIGH = lax.Precision.HIGHEST
F32 = jnp.float32
BF16 = jnp.bfloat16

C = 832
R = 1024
DEEP = ((0, 320), (320, 832))
EVEN = tuple((n, n + 208) for n in range(0, C, 208))
BLOCK = 64

HALF = C // 2
SMEM = pl.BlockSpec(memory_space=pltpu.SMEM)


def dot(first, second, dims=((1,), (0,)), precision=None):
    return lax.dot_general(first, second, (dims, ((), ())), precision=precision, preferred_element_type=F32)


def split(x):
    high = x.astype(BF16)
    return high, (x - high.astype(F32)).astype(BF16)


WHOLE = pl.BlockSpec(memory_space=pltpu.VMEM)
ANY = pl.BlockSpec(memory_space=pl.ANY)


def near(*arrays):
    return [pltpu.with_memory_space_constraint(x, pltpu.VMEM) for x in arrays]


def far(*arrays):
    return [pltpu.with_memory_space_constraint(x, pltpu.HBM) for x in arrays]


def params(mib):
    return pltpu.CompilerParams(vmem_limit_bytes=mib << 20)


def start_loads(sources, targets, groups, sems):
    copies = []
    for n, (start, stop) in enumerate(groups):
        rows = pl.ds(start, stop - start)
        pair = [
            pltpu.make_async_copy(source.at[rows], target.at[rows], sems.at[n, k])
            for k, (source, target) in enumerate(zip(sources, targets))
        ]
        for copy in pair:
            copy.start()
        copies.append(pair)
    return copies


def left_kernel(core_ref, m_hbm, g_hbm, r_hbm, left_ref, m_ref, g_ref, r_ref, both_ref, sum_ref, sems, r_sem):
    first = pltpu.make_async_copy(r_hbm, r_ref, r_sem)
    first.start()
    loads = start_loads((m_hbm, g_hbm), (m_ref, g_ref), DEEP, sems)
    first.wait()
    high, low = split(r_ref[...].T)
    both_ref[:RANK] = high
    both_ref[RANK:] = low
    for n, (start, stop) in enumerate(DEEP):
        for copy in loads[n]:
            copy.wait()
        high, low = split(m_ref[start:stop] + g_ref[start:stop].astype(F32))
        wide = dot(both_ref[:, start:stop], high)
        part = wide[:RANK] + wide[RANK:] + dot(both_ref[:RANK, start:stop], low)
        sum_ref[...] = part if n == 0 else sum_ref[...] + part
    left_ref[...] = sum_ref[...].T


def left_of(core, m, g, r):
    return pl.pallas_call(
        left_kernel,
        in_specs=[SMEM, ANY, ANY, ANY],
        out_specs=WHOLE,
        out_shape=pltpu.VMEM((R, RANK), F32),
        scratch_shapes=[
            pltpu.VMEM((C, R), F32),
            pltpu.VMEM((C, R), BF16),
            pltpu.VMEM((C, RANK), F32),
            pltpu.VMEM((2 * RANK, C), BF16),
            pltpu.VMEM((RANK, R), F32),
            pltpu.SemaphoreType.DMA((len(DEEP), 2)),
            pltpu.SemaphoreType.DMA,
        ],
        compiler_params=params(14),
        cost_estimate=pl.CostEstimate(flops=6 * R * C * RANK, bytes_accessed=R * C * 6, transcendentals=0),
        name="left_part",
    )(core, *far(m, g, r))


def spread_kernel(parts_ref, out_ref):
    out_ref[...] = jnp.broadcast_to(jnp.sum(parts_ref[...], axis=0, keepdims=True), out_ref.shape)


def sum_and_spread(parts, count):
    return pl.pallas_call(
        spread_kernel,
        out_shape=pltpu.VMEM((count,) + parts.shape[1:], F32),
        in_specs=[WHOLE],
        out_specs=WHOLE,
        compiler_params=params(4),
        cost_estimate=pl.CostEstimate(flops=parts.size, bytes_accessed=8 * parts.size, transcendentals=0),
        name="sum_and_spread",
    )(*near(parts))


def product(core_ref, away, both_ref, m_ref, g_ref, out_ref):
    base = (1 - core_ref[0] if away else core_ref[0]) * HALF
    for start in range(0, HALF, HALF // 2):
        rows = pl.ds(pl.multiple_of(base + start, 16), HALF // 2)
        high, low = split(m_ref[rows] + g_ref[rows].astype(F32))
        wide = dot(high, both_ref[...])
        out_ref[start : start + HALF // 2] = wide[:, :RANK] + wide[:, RANK:] + dot(low, both_ref[:, :RANK])


def give_kernel(core_ref, left_ref, m_ref, g_ref, give_ref, both_ref):
    left = left_ref[...]
    high, low = split(left)
    rest = (left - high.astype(F32) - low.astype(F32)).astype(BF16)
    both_ref[:, :RANK] = high
    both_ref[:, RANK:] = low
    wide = dot(high, both_ref[...], ((0,), (0,)))
    mixed = wide[:, RANK:] + dot(high, rest, ((0,), (0,)))
    give_ref[HALF:] = wide[:, :RANK] + (mixed + mixed.T + dot(low, low, ((0,), (0,))))
    product(core_ref, True, both_ref, m_ref, g_ref, give_ref)


def keep_kernel(core_ref, both_ref, m_ref, g_ref, give_ref, keep_ref):
    product(core_ref, False, both_ref, m_ref, g_ref, keep_ref)
    keep_ref[HALF:] = give_ref[HALF:]


def weighted_of(core, left, m, g):
    out = pltpu.VMEM((HALF + RANK, RANK), F32)
    cost = pl.CostEstimate(flops=3 * R * C * RANK, bytes_accessed=R * C * 3, transcendentals=0)
    give, both = pl.pallas_call(
        give_kernel,
        in_specs=[SMEM, WHOLE, WHOLE, WHOLE],
        out_specs=[WHOLE, WHOLE],
        out_shape=[out, pltpu.VMEM((R, 2 * RANK), BF16)],
        compiler_params=params(8),
        cost_estimate=cost,
        name="weighted_give",
    )(core, *near(left, m, g))
    keep = pl.pallas_call(
        keep_kernel,
        in_specs=[SMEM, WHOLE, WHOLE, WHOLE, WHOLE],
        out_specs=WHOLE,
        out_shape=out,
        compiler_params=params(8),
        cost_estimate=cost,
        name="weighted_keep",
    )(core, *near(both, m, g, give))
    return give, keep


def inverse_kernel(gram_ref, got_ref, out_ref, work_ref):
    n, b, t = RANK, BLOCK, 8
    row = lax.broadcasted_iota(jnp.int32, (n, n), 0)
    column = lax.broadcasted_iota(jnp.int32, (n, n), 1)
    work_ref[:, :n] = gram_ref[...] + got_ref[...]
    work_ref[:, n:] = jnp.where(row == column, 1.0, 0.0)
    place = lax.broadcasted_iota(jnp.int32, (t, n), 0)
    for o in range(0, n, b):
        upper = [work_ref[o + k : o + k + t, :n] for k in range(0, b, t)]
        inverse = [work_ref[o + k : o + k + t, n:] for k in range(0, b, t)]
        pivots = []
        for k in range(b // t):
            below = range(k, b // t)
            at = o + k * t
            columns = {q: [jnp.broadcast_to(upper[q][:, at + j : at + j + 1], (t, n)) for j in range(t)] for q in below}
            held = jnp.zeros((t, n), F32)
            for i in range(t):
                pivot = 1.0 / jnp.broadcast_to(columns[k][i][i : i + 1], (t, n))
                held = jnp.where(place == i, pivot, held)
                line = [columns[k][j][i : i + 1] for j in range(t)]
                upper_line, inverse_line = upper[k][i : i + 1], inverse[k][i : i + 1]
                for q in below:
                    factor = columns[q][i] * pivot
                    if q == k:
                        factor = jnp.where(place > i, factor, 0.0)
                    for j in range(i + 1, t):
                        columns[q][j] = columns[q][j] - factor * line[j]
                    upper[q] = upper[q] - factor * upper_line
                    inverse[q] = inverse[q] - factor * inverse_line
            pivots.append(held)
        root = jnp.sqrt(jnp.concatenate(pivots, axis=0))
        upper_block = jnp.concatenate(upper, axis=0) * root
        inverse_block = jnp.concatenate(inverse, axis=0) * root
        out_ref[o : o + b] = inverse_block
        if o + b < n:
            done = jnp.concatenate([upper_block, inverse_block], axis=1)
            work_ref[o + b :] -= dot(upper_block[:, o + b :], done, ((0,), (0,)), HIGH)


def inverse_of(gram, got):
    return pl.pallas_call(
        inverse_kernel,
        out_shape=pltpu.VMEM((RANK, RANK), F32),
        in_specs=[WHOLE, WHOLE],
        out_specs=WHOLE,
        scratch_shapes=[pltpu.VMEM((RANK, 2 * RANK), F32)],
        compiler_params=params(2),
        cost_estimate=pl.CostEstimate(flops=60 << 30, bytes_accessed=1 << 17, transcendentals=0),
        name="inverse_factor",
    )(*near(gram, got))


def across_kernel(part_ref, got_ref, inverse_ref, across_ref, colsq_ref):
    high, low = split(inverse_ref[...].T)
    three = jnp.concatenate([high, high, low], axis=0)
    high, low = split(part_ref[...] + got_ref[...])
    across = dot(jnp.concatenate([high, low, high], axis=1), three)
    across_ref[...] = across
    colsq_ref[...] = jnp.broadcast_to(jnp.sum(across * across, axis=0, keepdims=True), colsq_ref.shape)


def across_of(part, got, inverse):
    return pl.pallas_call(
        across_kernel,
        in_specs=[WHOLE, WHOLE, WHOLE],
        out_specs=[WHOLE, WHOLE],
        out_shape=[pltpu.VMEM((HALF, RANK), F32), pltpu.VMEM((64, RANK), F32)],
        compiler_params=params(4),
        cost_estimate=pl.CostEstimate(flops=6 * C * RANK * RANK, bytes_accessed=C * RANK * 8, transcendentals=0),
        name="across_part",
    )(*near(part, got, inverse))


def store(source, target, groups, sems, n):
    rows = pl.ds(groups[n][0], groups[n][1] - groups[n][0])
    copy = pltpu.make_async_copy(source.at[rows], target.at[rows], sems.at[n])
    copy.start()
    return copy


def momentum_kernel(
    core_ref, m_hbm, g_hbm, left_hbm, inverse_ref, mine_ref, other_ref,
    new_hbm, basis_ref, across_ref, m_ref, g_ref, left_ref, new_ref, sems, left_sem, out_sems,
):
    load = pltpu.make_async_copy(left_hbm, left_ref, left_sem)
    load.start()
    loads = start_loads((m_hbm, g_hbm), (m_ref, g_ref), EVEN, sems)
    high, low = split(inverse_ref[...])
    load.wait()
    both = split(left_ref[...])
    basis = dot(jnp.concatenate([high, high], axis=1), jnp.concatenate(both, axis=1), ((1,), (1,)))
    high, low = split(basis + dot(low, both[0], ((1,), (1,))))
    basis_ref[:RANK] = high
    basis_ref[RANK : 2 * RANK] = high
    basis_ref[2 * RANK :] = low
    mine = core_ref[0] * HALF
    across_ref[pl.ds(pl.multiple_of(mine, 8), HALF)] = mine_ref[...]
    across_ref[pl.ds(pl.multiple_of(HALF - mine, 8), HALF)] = other_ref[...]
    stores = []
    for n, (start, stop) in enumerate(EVEN):
        for copy in loads[n]:
            copy.wait()
        wide = jnp.concatenate(split(across_ref[start:stop] * 0.05), axis=1)
        blend = m_ref[start:stop] + g_ref[start:stop].astype(F32)
        new_ref[start:stop] = blend - dot(wide, basis_ref[: 2 * RANK])
        stores.append(store(new_ref, new_hbm, EVEN, out_sems, n))
    for copy in stores:
        copy.wait()


def momentum_of(core, m, g, left, inverse, mine, other):
    return pl.pallas_call(
        momentum_kernel,
        in_specs=[SMEM, ANY, ANY, ANY, WHOLE, WHOLE, WHOLE],
        out_specs=[ANY, WHOLE, WHOLE],
        out_shape=[pltpu.HBM((C, R), F32), pltpu.VMEM((3 * RANK, R), BF16), pltpu.VMEM((C, RANK), F32)],
        scratch_shapes=[
            pltpu.VMEM((C, R), F32),
            pltpu.VMEM((C, R), BF16),
            pltpu.VMEM((R, RANK), F32),
            pltpu.VMEM((C, R), F32),
            pltpu.SemaphoreType.DMA((len(EVEN), 2)),
            pltpu.SemaphoreType.DMA,
            pltpu.SemaphoreType.DMA((len(EVEN),)),
        ],
        compiler_params=params(14),
        cost_estimate=pl.CostEstimate(flops=1 << 20, bytes_accessed=1 << 16, transcendentals=0),
        name="new_momentum",
    )(core, *far(m, g), left, *near(inverse, mine, other))


def update_kernel(across_ref, colsq_ref, basis_ref, update_hbm, update_ref, sems):
    colsq = jnp.sum(colsq_ref[...], axis=0, keepdims=True)
    scale = (ROWS * COLS / RANK) ** 0.5 / jnp.sqrt(colsq + 1e-06)
    stores = []
    for n, (start, stop) in enumerate(EVEN):
        high, low = split(across_ref[start:stop] * scale)
        product = dot(jnp.concatenate([high, low, high], axis=1), basis_ref[...])
        update_ref[start:stop] = product.astype(BF16)
        stores.append(store(update_ref, update_hbm, EVEN, sems, n))
    for copy in stores:
        copy.wait()


def update_of(across, colsq, basis):
    return pl.pallas_call(
        update_kernel,
        in_specs=[WHOLE, WHOLE, WHOLE],
        out_specs=ANY,
        out_shape=pltpu.HBM((C, R), BF16),
        scratch_shapes=[pltpu.VMEM((C, R), BF16), pltpu.SemaphoreType.DMA((len(EVEN),))],
        compiler_params=params(6),
        cost_estimate=pl.CostEstimate(flops=6 * R * C * RANK, bytes_accessed=R * C * 2, transcendentals=0),
        name="update",
    )(*near(across, colsq, basis))


def exchange(blocks, axes):
    return lax.all_to_all(blocks, axes, 0, 0)


def swap_core(block):
    return lax.ppermute(block, "core", [(0, 1), (1, 0)])


def swap_y(block, step):
    pairs = [(i, i ^ 2 if i % 2 == step else 7 - (i ^ 1)) for i in range(8)]
    return lax.ppermute(block, ("y", "core"), pairs)


def body(momentum, gradient, right_factor):
    m, g = momentum.T, gradient.T
    core = lax.axis_index("core").astype(jnp.int32).reshape(1)
    partial = left_of(core, m, g, right_factor)
    quarter = sum_and_spread(exchange(partial.reshape(4, R // 4, RANK), "x"), 1)
    spread = sum_and_spread(exchange(quarter.reshape(8, R // 32, RANK), "z"), 32)
    left = exchange(spread, ("x", "z")).reshape(R, RANK)

    give, part = weighted_of(core, left, m, g)
    part = part + swap_core(give)
    part, gram = part[:HALF], part[HALF:]
    gram = gram + swap_y(gram, 0)
    inverse = inverse_of(gram, swap_y(gram, 1))
    part = part + swap_y(part, 0)
    mine, colsq = across_of(part, swap_y(part, 1), inverse)

    colsq = exchange(colsq.reshape(64, 1, RANK), ("core", "x", "z")).reshape(64, RANK)
    new_momentum, basis, across = momentum_of(core, m, g, left, inverse, mine, swap_core(mine))
    update = update_of(across, colsq, basis)
    return (new_momentum.T, update.T)


def solution(mesh):
    own = jax.sharding.Mesh(mesh.devices.reshape(4, 2, 4, 8), ("y", "core", "x", "z"))
    whole = P(("y", "core"), ("x", "z"))
    return jax.shard_map(
        body, mesh=own, in_specs=(whole, whole, P(("x", "z"), None)), out_specs=(whole, whole), check_vma=False
    )
```
